32 devices in a mesh: parts: 2 (over x), blk: 16 (over z, y, core).
Axes of the slice: x: 2, y: 2, z: 4, core: 2. Of those that a mesh axis runs over, the one named last changes fastest.
Arguments:
- queries: bfloat16 [512, 8192], P('blk'), may hold values from -6 to 6
- train_grads: bfloat16 [16384, 8192], P(('parts', 'blk')), parts along dimension 0, may hold values from -0.0625 to 0.0625
- group_of: int32 [8], replicated, may hold values from 0 to 7, each once
- basis_out: float32 [8, 32, 32], replicated, may hold values from -1 to 1
- basis_in: float32 [8, 32, 32], replicated, may hold values from -1 to 1
- eigen: float32 [8, 32, 32], replicated, may hold values from 0.1 to 10
- store_ids: int32 [16384], P('parts'), parts along dimension 0, may hold values from 0 to 8191, each once
Outputs:
- influence: bfloat16 [512, 16384], P('blk', 'parts'), parts along dimension 1
The draws below stay inside these ranges and needn't reach their ends.
There are 2 independent parts, one for each index of `parts`. The reference program is written for one: setup_inputs(seed, part) draws one part's arguments, and reference() takes and returns one part's arrays. A program takes and returns all parts, laid end to end along the dimension named above; an argument that names none is the same for every part. Nothing has to cross between parts.
Inputs may be any that keep to these rules, and one draw needn't show every extreme that they name: `group_of`: each layer group serves exactly one block. `store_ids`: every example id appears once.
All inputs are finite; a program needn't handle non-finite values.
Results may differ from the reference program's by a relative error of at most 0.0049.
Values may be sent and summed in bfloat16 or wider, within the bound.
A program may use at most 128 MiB of HBM per device.

```python
import math
import jax
import jax.numpy as jnp
from jax import lax

GROUPS = 8
SOUT = 32
SIN = 32
QUERIES = 512
TR_DEV = 512
FEAT = 8192
EXAMPLES = 8192
N_BLK = 16


def block_scale(key, extent, cuts, least, high):
    def one(axis_at, blocks):
        draws = jax.random.uniform(jax.random.fold_in(jax.random.fold_in(key, 6), axis_at), (blocks,), jnp.float32, least / len(cuts), high / len(cuts))
        return jnp.repeat(jnp.exp(draws), extent[axis_at] // blocks).reshape((-1,) + (1,) * (len(extent) - axis_at - 1))

    factor_of = one(*cuts[0])
    for cut in cuts[1:]:
        factor_of = factor_of * one(*cut)
    return factor_of


def bell_draw(rng, shape, width, limit, cuts=(), kind=jnp.bfloat16):
    array = jax.random.normal(rng, shape, jnp.float32) * width
    if len(cuts) > 0:
        array = block_scale(rng, shape, cuts, -0.22, 0.18) * array
    return jnp.clip(array, min=-limit, max=limit).astype(kind)


def setup_inputs(seed: int = 0, part: int = 0) -> dict:
    streams_of = jax.random.split(jax.random.key(seed), 8)
    own_keys = jax.random.split(jax.random.fold_in(streams_of[7], part), 8)
    queries = bell_draw(streams_of[0], (QUERIES, FEAT), 1.0, 6.0, ((0, 16),))
    train_grads = bell_draw(own_keys[1], (EXAMPLES, FEAT), FEAT ** -0.5, 0.0625, ((0, 16),))
    group_of = jax.random.permutation(streams_of[2], GROUPS).astype(jnp.int32)
    basis_out = bell_draw(streams_of[3], (GROUPS, SOUT, SOUT), SOUT ** -0.5, 1.0, (), jnp.float32)
    basis_in = bell_draw(streams_of[4], (GROUPS, SIN, SIN), SIN ** -0.5, 1.0, (), jnp.float32)
    eigen = jnp.clip(jnp.exp(jax.random.uniform(streams_of[5], (GROUPS, SOUT, SIN), jnp.float32, math.log(0.1), math.log(10.0))), 0.1, 10.0)
    store_ids = jax.random.permutation(own_keys[6], EXAMPLES).astype(jnp.int32)
    return dict(queries=queries, train_grads=train_grads, group_of=group_of, basis_out=basis_out, basis_in=basis_in, eigen=eigen, store_ids=store_ids)


damping_share = 0.1


def condition(query_rows, group_of, basis_out, basis_in, eigen):
    group_count, size_out, size_in = eigen.shape
    exact_mode = lax.Precision.HIGHEST
    chooser = (group_of[:, None] == jnp.arange(group_count, dtype=jnp.int32)[None, :]).astype(jnp.float32)
    damping = damping_share * jnp.mean(eigen, axis=(1, 2))
    basis_left = jnp.einsum('bg,gsi->bsi', chooser, basis_out, precision=exact_mode)
    basis_right = jnp.einsum('bg,gaj->baj', chooser, basis_in, precision=exact_mode)
    spectrum = jnp.einsum('bg,gij->bij', chooser, eigen + damping[:, None, None], precision=exact_mode)
    gradients = query_rows.astype(jnp.float32).reshape(query_rows.shape[0], group_count, size_out, size_in)
    rotated = jnp.einsum('bsi,qbsa->qbia', basis_left, gradients, precision=exact_mode)
    rotated = jnp.einsum('qbia,baj->qbij', rotated, basis_right, precision=exact_mode)
    scaled = rotated / spectrum[None]
    restored = jnp.einsum('bsi,qbij->qbsj', basis_left, scaled, precision=exact_mode)
    restored = jnp.einsum('qbsj,baj->qbsa', restored, basis_right, precision=exact_mode)
    return restored.reshape(query_rows.shape[0], group_count * size_out * size_in).astype(jnp.bfloat16)


def reference(queries, train_grads, group_of, basis_out, basis_in, eigen, store_ids):
    conditioned = condition(queries, group_of, basis_out, basis_in, eigen)
    ready = conditioned.astype(jnp.float32)
    slabs = train_grads.reshape(N_BLK, TR_DEV, FEAT)

    def score_slab(slab_rows):
        return jnp.dot(ready, slab_rows.astype(jnp.float32).T, precision=lax.Precision.HIGHEST, preferred_element_type=jnp.float32)

    blocks = lax.map(score_slab, slabs)
    scores = jnp.transpose(blocks, (1, 0, 2)).reshape(QUERIES, N_BLK * TR_DEV).astype(jnp.bfloat16)
    count = store_ids.shape[0]
    positions = jnp.zeros((count,), jnp.int32).at[store_ids].set(jnp.arange(count, dtype=jnp.int32))
    return jnp.take(scores, positions, axis=1)
```

```python
import functools

import jax
import jax.numpy as jnp
from jax import lax
from jax.experimental import pallas as pl
from jax.experimental.pallas import tpu as pltpu
from jax.sharding import PartitionSpec as P

damping_share = 0.1
LANES = 128
WIDE = 256


def pieces(values, count):
    parts = []
    for _ in range(count):
        part = values.astype(jnp.bfloat16)
        parts.append(part)
        values = values - part.astype(jnp.float32)
    return parts


def mxu(left, right):
    return lax.dot_general(
        left, right, (((1,), (0,)), ((), ())), preferred_element_type=jnp.float32
    )


def condition_kernel(order, group_ref, x_ref, bases_ref, eigen_ref, out_ref):
    del group_ref
    rows = x_ref.shape[0]
    per = LANES // order
    chunks = order // per
    bases = bases_ref[0]
    lane = lax.broadcasted_iota(jnp.int32, (order, order * order), 1)
    line = lax.broadcasted_iota(jnp.int32, (order, order * order), 0)
    spread = jnp.where(lane // order == line, 1.0, 0.0).astype(jnp.bfloat16)
    lane = lax.broadcasted_iota(jnp.int32, (order, LANES), 1)
    line = lax.broadcasted_iota(jnp.int32, (order, LANES), 0)
    repeat = jnp.where(lane % order == line, 1.0, 0.0).astype(jnp.bfloat16)

    first = 2 * order
    wide = mxu(jnp.concatenate(pieces(bases[:first], 3), axis=0), spread)
    wide = wide[:first] + wide[first : 2 * first] + wide[2 * first :]
    wide_out, wide_back = wide[:order], wide[order:]
    tall = mxu(jnp.concatenate(pieces(bases[first:], 2), axis=0), repeat)
    forward_high, back_high = tall[:order], tall[order : 2 * order]
    forward_low, back_low = tall[2 * order : 3 * order], tall[3 * order :]

    def placed(tile):
        blank = jnp.zeros_like(tile)
        return jnp.concatenate(
            [
                jnp.concatenate([tile if k == p else blank for k in range(per)], axis=0)
                for p in range(per)
            ],
            axis=1,
        ).astype(jnp.bfloat16)

    def mix(spread_rows, coefficients):
        totals = [jnp.zeros((rows, LANES), jnp.float32) for _ in range(chunks)]
        for c in range(chunks):
            for p in range(per):
                s = c * per + p
                value = spread_rows[c * rows : (c + 1) * rows, p * LANES : (p + 1) * LANES]
                for k in range(chunks):
                    weight = coefficients[s : s + 1, k * LANES : (k + 1) * LANES]
                    totals[k] = totals[k] + weight * value
        return totals

    x = x_ref[...].astype(jnp.float32)
    x = jnp.concatenate(
        [x[:, c * LANES : (c + 1) * LANES] for c in range(chunks)], axis=0
    ).astype(jnp.bfloat16)
    right = jnp.concatenate([placed(forward_high), placed(forward_low)], axis=0)
    rotated = mix(mxu(jnp.concatenate([x, x], axis=1), right), wide_out)

    eigen = eigen_ref[0]
    total = jnp.sum(jnp.sum(eigen, axis=1, keepdims=True), axis=0, keepdims=True)
    spectrum = eigen + damping_share * (total * (1.0 / (order * order)))
    scaled = jnp.concatenate(
        [rotated[k] / spectrum[k : k + 1] for k in range(chunks)], axis=0
    )
    high, low = pieces(scaled, 2)
    back = placed(back_high)
    restored = mxu(
        jnp.concatenate([high, low], axis=1), jnp.concatenate([back, back], axis=0)
    ) + mxu(high, placed(back_low))
    for k, total in enumerate(mix(restored, wide_back)):
        out_ref[:, k * LANES : (k + 1) * LANES] = total.astype(jnp.bfloat16)


def condition(queries, group_of, basis_out, basis_in, eigen):
    groups, order, _ = eigen.shape
    rows = queries.shape[0]
    size = order * order
    bases = jnp.concatenate(
        [basis_out, jnp.swapaxes(basis_out, 1, 2), basis_in, jnp.swapaxes(basis_in, 1, 2)],
        axis=1,
    )
    return pl.pallas_call(
        functools.partial(condition_kernel, order),
        grid_spec=pltpu.PrefetchScalarGridSpec(
            num_scalar_prefetch=1,
            grid=(groups,),
            in_specs=[
                pl.BlockSpec((rows, size), lambda b, g: (0, b)),
                pl.BlockSpec((1, 4 * order, order), lambda b, g: (g[b], 0, 0)),
                pl.BlockSpec((1, size // LANES, LANES), lambda b, g: (g[b], 0, 0)),
            ],
            out_specs=pl.BlockSpec((rows, size), lambda b, g: (0, b)),
        ),
        out_shape=jax.ShapeDtypeStruct(queries.shape, jnp.bfloat16),
        compiler_params=pltpu.CompilerParams(vmem_limit_bytes=32 * 1024 * 1024),
        name="condition",
    )(group_of, queries, bases, eigen.reshape(groups, size // LANES, LANES))


def arrange_kernel(scores_ref, ids_ref, out_ref, total):
    step = pl.program_id(0)
    rows, count = scores_ref.shape[1:]
    groups = out_ref.shape[1] // WIDE
    ids = ids_ref[0]
    coarse = ids // WIDE
    fine = ids % WIDE
    scores = scores_ref[0].astype(jnp.float32)
    left = jnp.concatenate(
        [jnp.where(coarse == h, scores, 0.0) for h in range(groups)], axis=0
    ).astype(jnp.bfloat16)
    line = lax.broadcasted_iota(jnp.int32, (WIDE, count), 0)
    chosen = jnp.where(line == fine, 1.0, 0.0).astype(jnp.bfloat16)
    term = lax.dot_general(
        left, chosen, (((1,), (1,)), ((), ())), preferred_element_type=jnp.float32
    )

    @pl.when(step == 0)
    def _():
        total[...] = term

    @pl.when(step > 0)
    def _():
        total[...] += term

    @pl.when(step == pl.num_programs(0) - 1)
    def _():
        for h in range(groups):
            out_ref[:, h * WIDE : (h + 1) * WIDE] = total[
                h * rows : (h + 1) * rows, :
            ].astype(jnp.bfloat16)


def arrange(parted, ids):
    blocks, rows, count = parted.shape
    width = blocks * count
    return pl.pallas_call(
        arrange_kernel,
        grid=(blocks,),
        in_specs=[
            pl.BlockSpec((1, rows, count), lambda k: (k, 0, 0)),
            pl.BlockSpec((1, 1, count), lambda k: (k, 0, 0)),
        ],
        out_specs=pl.BlockSpec((rows, width), lambda k: (0, 0)),
        out_shape=jax.ShapeDtypeStruct((rows, width), jnp.bfloat16),
        scratch_shapes=[pltpu.VMEM((rows * (width // WIDE), WIDE), jnp.float32)],
        compiler_params=pltpu.CompilerParams(vmem_limit_bytes=32 * 1024 * 1024),
        name="arrange",
    )(parted, ids.reshape(blocks, 1, count))


def local(queries, train_grads, group_of, basis_out, basis_in, eigen, store_ids):
    conditioned = condition(queries, group_of, basis_out, basis_in, eigen)
    scores = lax.dot_general(
        lax.all_gather(conditioned, "blk", axis=0, tiled=True),
        train_grads,
        (((1,), (1,)), ((), ())),
        preferred_element_type=jnp.float32,
    ).astype(jnp.bfloat16)
    blocks = scores.shape[0] // queries.shape[0]
    parted = lax.all_to_all(
        scores.reshape(blocks, queries.shape[0], scores.shape[1]),
        "blk",
        split_axis=0,
        concat_axis=0,
    )
    return arrange(parted, store_ids)


def solution(mesh):
    return jax.shard_map(
        local,
        mesh=mesh,
        in_specs=(P("blk", None), P(("parts", "blk"), None), P(), P(), P(), P(), P("parts")),
        out_specs=P("blk", "parts"),
        check_vma=False,
    )
```

```python
import functools

import jax
import jax.numpy as jnp
from jax import lax
from jax.experimental import pallas as pl
from jax.experimental.pallas import tpu as pltpu
from jax.sharding import PartitionSpec as P

damping_share = 0.1
LANES = 128
WIDE = 256


def pieces(values, count):
    parts = []
    for _ in range(count):
        part = values.astype(jnp.bfloat16)
        parts.append(part)
        values = values - part.astype(jnp.float32)
    return parts


def mxu(left, right):
    return lax.dot_general(
        left, right, (((1,), (0,)), ((), ())), preferred_element_type=jnp.float32
    )


def condition_kernel(order, group_ref, x_ref, bases_ref, eigen_ref, out_ref):
    del group_ref
    rows = x_ref.shape[0]
    per = LANES // order
    chunks = order // per
    bases = bases_ref[0]
    lane = lax.broadcasted_iota(jnp.int32, (order, order * order), 1)
    line = lax.broadcasted_iota(jnp.int32, (order, order * order), 0)
    spread = jnp.where(lane // order == line, 1.0, 0.0).astype(jnp.bfloat16)
    lane = lax.broadcasted_iota(jnp.int32, (order, LANES), 1)
    line = lax.broadcasted_iota(jnp.int32, (order, LANES), 0)
    repeat = jnp.where(lane % order == line, 1.0, 0.0).astype(jnp.bfloat16)

    first = 2 * order
    wide = mxu(jnp.concatenate(pieces(bases[:first], 3), axis=0), spread)
    wide = wide[:first] + wide[first : 2 * first] + wide[2 * first :]
    wide_out, wide_back = wide[:order], wide[order:]
    tall = mxu(jnp.concatenate(pieces(bases[first:], 2), axis=0), repeat)
    forward_high, back_high = tall[:order], tall[order : 2 * order]
    forward_low, back_low = tall[2 * order : 3 * order], tall[3 * order :]

    def placed(tile):
        blank = jnp.zeros_like(tile)
        return jnp.concatenate(
            [
                jnp.concatenate([tile if k == p else blank for k in range(per)], axis=0)
                for p in range(per)
            ],
            axis=1,
        ).astype(jnp.bfloat16)

    def mix(spread_rows, coefficients):
        totals = [jnp.zeros((rows, LANES), jnp.float32) for _ in range(chunks)]
        for c in range(chunks):
            for p in range(per):
                s = c * per + p
                value = spread_rows[c * rows : (c + 1) * rows, p * LANES : (p + 1) * LANES]
                for k in range(chunks):
                    weight = coefficients[s : s + 1, k * LANES : (k + 1) * LANES]
                    totals[k] = totals[k] + weight * value
        return totals

    x = x_ref[...].astype(jnp.float32)
    x = jnp.concatenate(
        [x[:, c * LANES : (c + 1) * LANES] for c in range(chunks)], axis=0
    ).astype(jnp.bfloat16)
    right = jnp.concatenate([placed(forward_high), placed(forward_low)], axis=0)
    rotated = mix(mxu(jnp.concatenate([x, x], axis=1), right), wide_out)

    eigen = eigen_ref[0]
    total = jnp.sum(jnp.sum(eigen, axis=1, keepdims=True), axis=0, keepdims=True)
    spectrum = eigen + damping_share * (total * (1.0 / (order * order)))
    scaled = jnp.concatenate(
        [rotated[k] / spectrum[k : k + 1] for k in range(chunks)], axis=0
    )
    high, low = pieces(scaled, 2)
    back = placed(back_high)
    restored = mxu(
        jnp.concatenate([high, low], axis=1), jnp.concatenate([back, back], axis=0)
    ) + mxu(high, placed(back_low))
    for k, total in enumerate(mix(restored, wide_back)):
        out_ref[:, k * LANES : (k + 1) * LANES] = total.astype(jnp.bfloat16)


def condition(queries, group_of, basis_out, basis_in, eigen):
    groups, order, _ = eigen.shape
    rows = queries.shape[0]
    size = order * order
    bases = jnp.concatenate(
        [basis_out, jnp.swapaxes(basis_out, 1, 2), basis_in, jnp.swapaxes(basis_in, 1, 2)],
        axis=1,
    )
    return pl.pallas_call(
        functools.partial(condition_kernel, order),
        grid_spec=pltpu.PrefetchScalarGridSpec(
            num_scalar_prefetch=1,
            grid=(groups,),
            in_specs=[
                pl.BlockSpec((rows, size), lambda b, g: (0, b)),
                pl.BlockSpec((1, 4 * order, order), lambda b, g: (g[b], 0, 0)),
                pl.BlockSpec((1, size // LANES, LANES), lambda b, g: (g[b], 0, 0)),
            ],
            out_specs=pl.BlockSpec((rows, size), lambda b, g: (0, b)),
        ),
        out_shape=jax.ShapeDtypeStruct(queries.shape, jnp.bfloat16),
        compiler_params=pltpu.CompilerParams(vmem_limit_bytes=32 * 1024 * 1024),
        name="condition",
    )(group_of, queries, bases, eigen.reshape(groups, size // LANES, LANES))


def arrange_kernel(scores_ref, ids_ref, out_ref, total):
    step = pl.program_id(0)
    rows, count = scores_ref.shape[1:]
    groups = out_ref.shape[1] // WIDE
    ids = ids_ref[0]
    coarse = ids // WIDE
    fine = ids % WIDE
    scores = scores_ref[0].astype(jnp.float32)
    left = jnp.concatenate(
        [jnp.where(coarse == h, scores, 0.0) for h in range(groups)], axis=0
    ).astype(jnp.bfloat16)
    line = lax.broadcasted_iota(jnp.int32, (WIDE, count), 0)
    chosen = jnp.where(line == fine, 1.0, 0.0).astype(jnp.bfloat16)
    term = lax.dot_general(
        left, chosen, (((1,), (1,)), ((), ())), preferred_element_type=jnp.float32
    )

    @pl.when(step == 0)
    def _():
        total[...] = term

    @pl.when(step > 0)
    def _():
        total[...] += term

    @pl.when(step == pl.num_programs(0) - 1)
    def _():
        for h in range(groups):
            out_ref[:, h * WIDE : (h + 1) * WIDE] = total[
                h * rows : (h + 1) * rows, :
            ].astype(jnp.bfloat16)


def arrange(parted, ids):
    blocks, rows, count = parted.shape
    width = blocks * count
    return pl.pallas_call(
        arrange_kernel,
        grid=(blocks,),
        in_specs=[
            pl.BlockSpec((1, rows, count), lambda k: (k, 0, 0)),
            pl.BlockSpec((1, 1, count), lambda k: (k, 0, 0)),
        ],
        out_specs=pl.BlockSpec((rows, width), lambda k: (0, 0)),
        out_shape=jax.ShapeDtypeStruct((rows, width), jnp.bfloat16),
        scratch_shapes=[pltpu.VMEM((rows * (width // WIDE), WIDE), jnp.float32)],
        compiler_params=pltpu.CompilerParams(vmem_limit_bytes=32 * 1024 * 1024),
        name="arrange",
    )(parted, ids.reshape(blocks, 1, count))


def ring_kernel(cores, x_ref, train_hbm, out_ref, held, train, total, stage, train_sem,
                ring_send, ring_recv, twin_send, twin_recv, back_send, back_recv):
    blocks, rows, count = out_ref.shape
    half = rows // 2
    depth = x_ref.shape[1]
    chips = blocks // cores
    long = chips // 2
    subs = 2
    part = depth // subs
    quanta = 4
    slice_of = depth // quanta
    step_rows = 4 * half
    pair = 2 * step_rows
    me = lax.axis_index("blk")
    core = me % cores
    chip = me // cores
    deep, side = chip // 2, chip % 2
    place = deep + side * (2 * long - 1 - 2 * deep)

    def device(position, its_core):
        at_side = position // long
        at_deep = position + at_side * (2 * long - 1 - 2 * position)
        return (at_deep * 2 + at_side) * cores + its_core

    onward = [device((place + 1) % chips, core), device((place + chips - 1) % chips, core)]
    twin = device(place, 1 - core)

    def rows_of(t, d, k):
        return pl.ds(pl.multiple_of((t * 4 + d * 2 + k) * half, half), half)

    def ring_copy(t, d, u):
        columns = pl.ds(u * part, part)
        return pltpu.make_async_remote_copy(
            src_ref=held.at[rows_of(t, d, 0), columns],
            dst_ref=held.at[rows_of(t + 1, d, 0), columns],
            send_sem=ring_send.at[t, d, u],
            recv_sem=ring_recv.at[t, d, u],
            device_id={"blk": onward[d]},
            device_id_type=pl.DeviceIdType.MESH,
        )

    def twin_copy(t, d, u):
        columns = pl.ds(u * part, part)
        return pltpu.make_async_remote_copy(
            src_ref=held.at[rows_of(t, d, 0), columns],
            dst_ref=held.at[rows_of(t, d, 1), columns],
            send_sem=twin_send.at[t, d, u],
            recv_sem=twin_recv.at[t, d, u],
            device_id={"blk": twin},
            device_id_type=pl.DeviceIdType.MESH,
        )

    def back_copy(t, d, k):
        shift = t if d == 1 else chips - t
        owner = device((place + shift) % chips, core if k == 0 else 1 - core)
        return pltpu.make_async_remote_copy(
            src_ref=stage.at[rows_of(t, d, k)],
            dst_ref=out_ref.at[me, pl.ds(d * half, half)],
            send_sem=back_send.at[t, d, k],
            recv_sem=back_recv.at[t, d, k],
            device_id={"blk": owner},
            device_id_type=pl.DeviceIdType.MESH,
        )

    load = pltpu.make_async_copy(train_hbm, train, train_sem)
    load.start()
    barrier = pltpu.get_barrier_semaphore()

    @pl.loop(1, blocks)
    def _(k):
        pl.semaphore_signal(
            barrier, inc=1, device_id={"blk": (me + k) % blocks},
            device_id_type=pl.DeviceIdType.MESH,
        )

    for d in range(2):
        held[pl.ds(d * 2 * half, half), :] = x_ref[pl.ds(d * half, half), :]
    pl.semaphore_wait(barrier, blocks - 1)

    def multiply(g, q):
        if q % (quanta // subs) == 0:
            for step in range(2):
                for d in range(2):
                    twin_copy(g * 2 + step, d, q // (quanta // subs)).wait_recv()
        columns = pl.ds(q * slice_of, slice_of)
        base = pl.ds(pl.multiple_of(g * pair, pair), pair)
        term = lax.dot_general(
            held[base, columns], train[:, columns], (((1,), (1,)), ((), ())),
            preferred_element_type=jnp.float32,
        )
        if q == 0:
            total[...] = term
        elif q < quanta - 1:
            total[...] += term
        else:
            stage[base, :] = (total[...] + term).astype(jnp.bfloat16)
            for step in range(2):
                for d in range(2):
                    for k in range(2):
                        if step == 0 and k == 0:

                            @pl.when(g > 0)
                            def _():
                                back_copy(g * 2 + step, d, k).start()

                        else:
                            back_copy(g * 2 + step, d, k).start()

    @pl.loop(0, chips // 2)
    def _(g):
        for step in range(2):
            t = g * 2 + step
            for u in range(subs):
                for d in range(2):
                    if step == 0:

                        @pl.when(g > 0)
                        def _():
                            ring_copy(t - 1, d, u).wait_recv()

                    else:
                        ring_copy(t - 1, d, u).wait_recv()
                    if step == 1:

                        @pl.when(g < chips // 2 - 1)
                        def _():
                            ring_copy(t, d, u).start()

                    else:
                        ring_copy(t, d, u).start()
                    twin_copy(t, d, u).start()

                @pl.when(g > 0)
                def _():
                    @pl.when(g == 1)
                    def _():
                        if step == 0 and u == 0:
                            load.wait()

                    multiply(g - 1, step * subs + u)

    for q in range(quanta):
        multiply(chips // 2 - 1, q)
    for d in range(2):
        out_ref[me, pl.ds(d * half, half), :] = stage[pl.ds(d * 2 * half, half), :]

    @pl.loop(0, chips)
    def _(t):
        for d in range(2):
            for u in range(subs):
                twin_copy(t, d, u).wait_send()

                @pl.when(t < chips - 1)
                def _():
                    ring_copy(t, d, u).wait_send()

            back_copy(t, d, 1).wait()

            @pl.when(t > 0)
            def _():
                back_copy(t, d, 0).wait()


def ring_scores(conditioned, train_grads, blocks, cores):
    rows, depth = conditioned.shape
    count = train_grads.shape[0]
    steps = blocks // cores
    return pl.pallas_call(
        functools.partial(ring_kernel, cores),
        out_shape=jax.ShapeDtypeStruct((blocks, rows, count), jnp.bfloat16),
        in_specs=[
            pl.BlockSpec(memory_space=pltpu.VMEM),
            pl.BlockSpec(memory_space=pl.ANY),
        ],
        out_specs=pl.BlockSpec(memory_space=pltpu.VMEM),
        scratch_shapes=[
            pltpu.VMEM((blocks * rows, depth), jnp.bfloat16),
            pltpu.VMEM((count, depth), jnp.bfloat16),
            pltpu.VMEM((4 * rows, count), jnp.float32),
            pltpu.VMEM((blocks * rows, count), jnp.bfloat16),
            pltpu.SemaphoreType.DMA,
            pltpu.SemaphoreType.DMA((steps, 2, 2)),
            pltpu.SemaphoreType.DMA((steps, 2, 2)),
            pltpu.SemaphoreType.DMA((steps, 2, 2)),
            pltpu.SemaphoreType.DMA((steps, 2, 2)),
            pltpu.SemaphoreType.DMA((steps, 2, 2)),
            pltpu.SemaphoreType.DMA((steps, 2, 2)),
        ],
        compiler_params=pltpu.CompilerParams(
            collective_id=0, has_side_effects=True, vmem_limit_bytes=40 * 1024 * 1024
        ),
        name="ring_scores",
    )(conditioned, train_grads)


def plain_scores(conditioned, train_grads):
    scores = lax.dot_general(
        lax.all_gather(conditioned, "blk", axis=0, tiled=True),
        train_grads,
        (((1,), (1,)), ((), ())),
        preferred_element_type=jnp.float32,
    ).astype(jnp.bfloat16)
    rows = conditioned.shape[0]
    return lax.all_to_all(
        scores.reshape(scores.shape[0] // rows, rows, scores.shape[1]),
        "blk",
        split_axis=0,
        concat_axis=0,
    )


def local(blocks, queries, train_grads, group_of, basis_out, basis_in, eigen, store_ids):
    conditioned = condition(queries, group_of, basis_out, basis_in, eigen)
    if blocks == 16 and queries.shape[0] % 32 == 0:
        parted = ring_scores(conditioned, train_grads, blocks, 2)
    else:
        parted = plain_scores(conditioned, train_grads)
    return arrange(parted, store_ids)


def solution(mesh):
    return jax.shard_map(
        functools.partial(local, mesh.shape["blk"]),
        mesh=mesh,
        in_specs=(P("blk", None), P(("parts", "blk"), None), P(), P(), P(), P(), P("parts")),
        out_specs=P("blk", "parts"),
        check_vma=False,
    )
```

```python
import functools

import jax
import jax.numpy as jnp
from jax import lax
from jax.experimental import pallas as pl
from jax.experimental.pallas import tpu as pltpu
from jax.sharding import PartitionSpec as P

damping_share = 0.1
LANES = 128
WIDE = 256


def pieces(values, count):
    parts = []
    for _ in range(count):
        part = values.astype(jnp.bfloat16)
        parts.append(part)
        values = values - part.astype(jnp.float32)
    return parts


def mxu(left, right):
    return lax.dot_general(
        left, right, (((1,), (0,)), ((), ())), preferred_element_type=jnp.float32
    )


def condition_kernel(order, group_ref, x_ref, bases_ref, eigen_ref, out_ref):
    del group_ref
    rows = x_ref.shape[0]
    per = LANES // order
    chunks = order // per
    bases = bases_ref[0]
    lane = lax.broadcasted_iota(jnp.int32, (order, order * order), 1)
    line = lax.broadcasted_iota(jnp.int32, (order, order * order), 0)
    spread = jnp.where(lane // order == line, 1.0, 0.0).astype(jnp.bfloat16)
    lane = lax.broadcasted_iota(jnp.int32, (order, LANES), 1)
    line = lax.broadcasted_iota(jnp.int32, (order, LANES), 0)
    repeat = jnp.where(lane % order == line, 1.0, 0.0).astype(jnp.bfloat16)

    first = 2 * order
    wide = mxu(jnp.concatenate(pieces(bases[:first], 3), axis=0), spread)
    wide = wide[:first] + wide[first : 2 * first] + wide[2 * first :]
    wide_out, wide_back = wide[:order], wide[order:]
    tall = mxu(jnp.concatenate(pieces(bases[first:], 2), axis=0), repeat)
    forward_high, back_high = tall[:order], tall[order : 2 * order]
    forward_low, back_low = tall[2 * order : 3 * order], tall[3 * order :]

    def placed(tile):
        blank = jnp.zeros_like(tile)
        return jnp.concatenate(
            [
                jnp.concatenate([tile if k == p else blank for k in range(per)], axis=0)
                for p in range(per)
            ],
            axis=1,
        ).astype(jnp.bfloat16)

    def mix(spread_rows, coefficients):
        totals = [jnp.zeros((rows, LANES), jnp.float32) for _ in range(chunks)]
        for c in range(chunks):
            for p in range(per):
                s = c * per + p
                value = spread_rows[c * rows : (c + 1) * rows, p * LANES : (p + 1) * LANES]
                for k in range(chunks):
                    weight = coefficients[s : s + 1, k * LANES : (k + 1) * LANES]
                    totals[k] = totals[k] + weight * value
        return totals

    x = x_ref[...].astype(jnp.float32)
    x = jnp.concatenate(
        [x[:, c * LANES : (c + 1) * LANES] for c in range(chunks)], axis=0
    ).astype(jnp.bfloat16)
    right = jnp.concatenate([placed(forward_high), placed(forward_low)], axis=0)
    rotated = mix(mxu(jnp.concatenate([x, x], axis=1), right), wide_out)

    eigen = eigen_ref[0]
    total = jnp.sum(jnp.sum(eigen, axis=1, keepdims=True), axis=0, keepdims=True)
    spectrum = eigen + damping_share * (total * (1.0 / (order * order)))
    scaled = jnp.concatenate(
        [rotated[k] / spectrum[k : k + 1] for k in range(chunks)], axis=0
    )
    high, low = pieces(scaled, 2)
    back = placed(back_high)
    restored = mxu(
        jnp.concatenate([high, low], axis=1), jnp.concatenate([back, back], axis=0)
    ) + mxu(high, placed(back_low))
    for k, total in enumerate(mix(restored, wide_back)):
        out_ref[:, k * LANES : (k + 1) * LANES] = total.astype(jnp.bfloat16)


def condition(queries, group_of, basis_out, basis_in, eigen):
    groups, order, _ = eigen.shape
    rows = queries.shape[0]
    size = order * order
    bases = jnp.concatenate(
        [basis_out, jnp.swapaxes(basis_out, 1, 2), basis_in, jnp.swapaxes(basis_in, 1, 2)],
        axis=1,
    )
    return pl.pallas_call(
        functools.partial(condition_kernel, order),
        grid_spec=pltpu.PrefetchScalarGridSpec(
            num_scalar_prefetch=1,
            grid=(groups,),
            in_specs=[
                pl.BlockSpec((rows, size), lambda b, g: (0, b)),
                pl.BlockSpec((1, 4 * order, order), lambda b, g: (g[b], 0, 0)),
                pl.BlockSpec((1, size // LANES, LANES), lambda b, g: (g[b], 0, 0)),
            ],
            out_specs=pl.BlockSpec((rows, size), lambda b, g: (0, b)),
        ),
        out_shape=jax.ShapeDtypeStruct(queries.shape, jnp.bfloat16),
        compiler_params=pltpu.CompilerParams(vmem_limit_bytes=32 * 1024 * 1024),
        name="condition",
    )(group_of, queries, bases, eigen.reshape(groups, size // LANES, LANES))


def arrange_kernel(scores_ref, ids_ref, out_ref, total):
    step = pl.program_id(0)
    taken, rows, count = scores_ref.shape
    groups = out_ref.shape[1] // WIDE
    ids = jnp.concatenate([ids_ref[k] for k in range(taken)], axis=1)
    coarse = ids // WIDE
    fine = ids % WIDE
    scores = jnp.concatenate([scores_ref[k] for k in range(taken)], axis=1).astype(
        jnp.float32
    )
    left = jnp.concatenate(
        [jnp.where(coarse == h, scores, 0.0) for h in range(groups)], axis=0
    ).astype(jnp.bfloat16)
    line = lax.broadcasted_iota(jnp.int32, (WIDE, taken * count), 0)
    chosen = jnp.where(line == fine, 1.0, 0.0).astype(jnp.bfloat16)
    term = lax.dot_general(
        left, chosen, (((1,), (1,)), ((), ())), preferred_element_type=jnp.float32
    )

    @pl.when(step == 0)
    def _():
        total[...] = term

    @pl.when(step > 0)
    def _():
        total[...] += term

    @pl.when(step == pl.num_programs(0) - 1)
    def _():
        for h in range(groups):
            out_ref[:, h * WIDE : (h + 1) * WIDE] = total[
                h * rows : (h + 1) * rows, :
            ].astype(jnp.bfloat16)


def arrange(parted, ids):
    blocks, rows, count = parted.shape
    width = blocks * count
    taken = 4 if blocks % 4 == 0 else 1
    return pl.pallas_call(
        arrange_kernel,
        grid=(blocks // taken,),
        in_specs=[
            pl.BlockSpec((taken, rows, count), lambda k: (k, 0, 0)),
            pl.BlockSpec((taken, 1, count), lambda k: (k, 0, 0)),
        ],
        out_specs=pl.BlockSpec((rows, width), lambda k: (0, 0)),
        out_shape=jax.ShapeDtypeStruct((rows, width), jnp.bfloat16),
        scratch_shapes=[pltpu.VMEM((rows * (width // WIDE), WIDE), jnp.float32)],
        compiler_params=pltpu.CompilerParams(vmem_limit_bytes=32 * 1024 * 1024),
        name="arrange",
    )(parted, ids.reshape(blocks, 1, count))


def ring_kernel(cores, x_ref, train_hbm, out_ref, held, train, total, stage, train_sem,
                ring_send, ring_recv, twin_send, twin_recv, back_send, back_recv,
                side_send, side_recv):
    blocks, rows, count = out_ref.shape
    half = rows // 2
    depth = x_ref.shape[1]
    chips = blocks // cores
    long = chips // 2
    third = (depth // 3 + WIDE // 2) // WIDE * WIDE
    slab = lax.axis_index("parts")
    step_rows = 4 * half
    pair = 2 * step_rows
    me = lax.axis_index("blk")
    core = me % cores
    chip = me // cores
    deep, side = chip // 2, chip % 2
    place = deep + side * (2 * long - 1 - 2 * deep)

    def device(position, its_core):
        at_side = position // long
        at_deep = position + at_side * (2 * long - 1 - 2 * position)
        return (at_deep * 2 + at_side) * cores + its_core

    onward = [device((place + 1) % chips, core), device((place + chips - 1) % chips, core)]
    twin = device(place, 1 - core)

    def columns_of(u):
        if u == 1:
            return pl.ds(2 * third, depth - 2 * third)
        start = slab if u == 0 else 1 - slab
        return pl.ds(pl.multiple_of(start * third, WIDE), third)

    def rows_of(t, d, k):
        return pl.ds(pl.multiple_of((t * 4 + d * 2 + k) * half, half), half)

    def ring_copy(t, d, u):
        columns = columns_of(u)
        return pltpu.make_async_remote_copy(
            src_ref=held.at[rows_of(t, d, 0), columns],
            dst_ref=held.at[rows_of(t + 1, d, 0), columns],
            send_sem=ring_send.at[t, d, u],
            recv_sem=ring_recv.at[t, d, u],
            device_id={"blk": onward[d]},
            device_id_type=pl.DeviceIdType.MESH,
        )

    def twin_copy(t, d, u):
        columns = columns_of(u)
        return pltpu.make_async_remote_copy(
            src_ref=held.at[rows_of(t, d, 0), columns],
            dst_ref=held.at[rows_of(t, d, 1), columns],
            send_sem=twin_send.at[t, d, u],
            recv_sem=twin_recv.at[t, d, u],
            device_id={"blk": twin},
            device_id_type=pl.DeviceIdType.MESH,
        )

    def side_copy(t, d):
        columns = columns_of(0)
        return pltpu.make_async_remote_copy(
            src_ref=held.at[rows_of(t, d, 0), columns],
            dst_ref=held.at[rows_of(t, d, 0), columns],
            send_sem=side_send.at[t, d],
            recv_sem=side_recv.at[t, d],
            device_id={"parts": 1 - slab},
            device_id_type=pl.DeviceIdType.MESH,
        )

    def back_copy(t, d, k):
        shift = t if d == 1 else chips - t
        owner = device((place + shift) % chips, core if k == 0 else 1 - core)
        return pltpu.make_async_remote_copy(
            src_ref=stage.at[rows_of(t, d, k)],
            dst_ref=out_ref.at[me, pl.ds(d * half, half)],
            send_sem=back_send.at[t, d, k],
            recv_sem=back_recv.at[t, d, k],
            device_id={"blk": owner},
            device_id_type=pl.DeviceIdType.MESH,
        )

    load = pltpu.make_async_copy(train_hbm, train, train_sem)
    load.start()
    barrier = pltpu.get_barrier_semaphore()

    @pl.loop(1, blocks)
    def _(k):
        pl.semaphore_signal(
            barrier, inc=1, device_id={"blk": (me + k) % blocks},
            device_id_type=pl.DeviceIdType.MESH,
        )

    pl.semaphore_signal(
        barrier, inc=1, device_id={"parts": 1 - slab},
        device_id_type=pl.DeviceIdType.MESH,
    )
    for d in range(2):
        held[pl.ds(d * 2 * half, half), :] = x_ref[pl.ds(d * half, half), :]
    pl.semaphore_wait(barrier, blocks)

    def multiply(g, q):
        for step in range(2):
            for d in range(2):
                twin_copy(g * 2 + step, d, q).wait_recv()
        columns = columns_of(q)
        base = pl.ds(pl.multiple_of(g * pair, pair), pair)
        term = lax.dot_general(
            held[base, columns], train[:, columns], (((1,), (1,)), ((), ())),
            preferred_element_type=jnp.float32,
        )
        if q == 0:
            total[...] = term
        elif q == 1:
            total[...] += term
        else:
            stage[base, :] = (total[...] + term).astype(jnp.bfloat16)
            for step in range(2):
                for d in range(2):
                    for k in range(2):
                        if step == 0 and k == 0:

                            @pl.when(g > 0)
                            def _():
                                back_copy(g * 2 + step, d, k).start()

                        else:
                            back_copy(g * 2 + step, d, k).start()

    def from_side(t):
        for d in range(2):
            side_copy(t, d).wait_recv()
            twin_copy(t, d, 2).start()

    def forward(t, d, u):
        ring_copy(t, d, u).start()

    last = chips // 2 - 1

    @pl.loop(0, chips // 2)
    def _(g):
        for step in range(2):
            t = g * 2 + step
            for u in range(2):
                for d in range(2):
                    if step == 0:

                        @pl.when(g > 0)
                        def _():
                            ring_copy(t - 1, d, u).wait_recv()

                        forward(t, d, u)
                    else:
                        ring_copy(t - 1, d, u).wait_recv()

                        @pl.when(g < last)
                        def _():
                            forward(t, d, u)

                    if u == 0:
                        if step == 0:

                            @pl.when(g > 0)
                            def _():
                                side_copy(t, d).start()

                        else:
                            side_copy(t, d).start()
                    twin_copy(t, d, u).start()
                if step == 0:

                    @pl.when(g > 0)
                    def _():
                        if u == 0:

                            @pl.when(g == 1)
                            def _():
                                load.wait()

                        multiply(g - 1, u)

                elif u == 0:

                    @pl.when(g > 0)
                    def _():
                        multiply(g - 1, 2)

            if step == 0:

                @pl.when(g == 0)
                def _():
                    for d in range(2):
                        twin_copy(t, d, 2).start()

                @pl.when(g > 0)
                def _():
                    from_side(t - 1)

            else:

                @pl.when(g > 0)
                def _():
                    from_side(t - 1)

    multiply(last, 0)
    multiply(last, 1)
    from_side(chips - 1)
    multiply(last, 2)
    for d in range(2):
        out_ref[me, pl.ds(d * half, half), :] = stage[pl.ds(d * 2 * half, half), :]

    @pl.loop(0, chips)
    def _(t):
        for d in range(2):
            for u in range(3):
                twin_copy(t, d, u).wait_send()
            for u in range(2):

                @pl.when(t < chips - 1)
                def _():
                    ring_copy(t, d, u).wait_send()

            back_copy(t, d, 1).wait()

            @pl.when(t > 0)
            def _():
                side_copy(t, d).wait_send()
                back_copy(t, d, 0).wait()


def ring_scores(conditioned, train_grads, blocks, cores):
    rows, depth = conditioned.shape
    count = train_grads.shape[0]
    steps = blocks // cores
    return pl.pallas_call(
        functools.partial(ring_kernel, cores),
        out_shape=jax.ShapeDtypeStruct((blocks, rows, count), jnp.bfloat16),
        in_specs=[
            pl.BlockSpec(memory_space=pltpu.VMEM),
            pl.BlockSpec(memory_space=pl.ANY),
        ],
        out_specs=pl.BlockSpec(memory_space=pltpu.VMEM),
        scratch_shapes=[
            pltpu.VMEM((blocks * rows, depth), jnp.bfloat16),
            pltpu.VMEM((count, depth), jnp.bfloat16),
            pltpu.VMEM((4 * rows, count), jnp.float32),
            pltpu.VMEM((blocks * rows, count), jnp.bfloat16),
            pltpu.SemaphoreType.DMA,
            pltpu.SemaphoreType.DMA((steps, 2, 2)),
            pltpu.SemaphoreType.DMA((steps, 2, 2)),
            pltpu.SemaphoreType.DMA((steps, 2, 3)),
            pltpu.SemaphoreType.DMA((steps, 2, 3)),
            pltpu.SemaphoreType.DMA((steps, 2, 2)),
            pltpu.SemaphoreType.DMA((steps, 2, 2)),
            pltpu.SemaphoreType.DMA((steps, 2)),
            pltpu.SemaphoreType.DMA((steps, 2)),
        ],
        compiler_params=pltpu.CompilerParams(
            collective_id=0, has_side_effects=True, vmem_limit_bytes=56 * 1024 * 1024
        ),
        name="ring_scores",
    )(conditioned, train_grads)


def plain_scores(conditioned, train_grads):
    scores = lax.dot_general(
        lax.all_gather(conditioned, "blk", axis=0, tiled=True),
        train_grads,
        (((1,), (1,)), ((), ())),
        preferred_element_type=jnp.float32,
    ).astype(jnp.bfloat16)
    rows = conditioned.shape[0]
    return lax.all_to_all(
        scores.reshape(scores.shape[0] // rows, rows, scores.shape[1]),
        "blk",
        split_axis=0,
        concat_axis=0,
    )


def local(parts, blocks, queries, train_grads, group_of, basis_out, basis_in, eigen, store_ids):
    conditioned = condition(queries, group_of, basis_out, basis_in, eigen)
    if parts == 2 and blocks == 16 and queries.shape[0] % 32 == 0:
        parted = ring_scores(conditioned, train_grads, blocks, 2)
    else:
        parted = plain_scores(conditioned, train_grads)
    return arrange(parted, store_ids)


def solution(mesh):
    return jax.shard_map(
        functools.partial(local, mesh.shape["parts"], mesh.shape["blk"]),
        mesh=mesh,
        in_specs=(P("blk", None), P(("parts", "blk"), None), P(), P(), P(), P(), P("parts")),
        out_specs=P("blk", "parts"),
        check_vma=False,
    )
```

```python
import functools

import jax
import jax.numpy as jnp
from jax import lax
from jax.experimental import pallas as pl
from jax.experimental.pallas import tpu as pltpu
from jax.sharding import PartitionSpec as P

damping_share = 0.1
LANES = 128
WIDE = 256


def pieces(values, count):
    parts = []
    for _ in range(count):
        part = values.astype(jnp.bfloat16)
        parts.append(part)
        values = values - part.astype(jnp.float32)
    return parts


def mxu(left, right):
    return lax.dot_general(
        left, right, (((1,), (0,)), ((), ())), preferred_element_type=jnp.float32
    )


def condition_kernel(order, group_ref, x_ref, output_ref, input_ref, eigen_ref, out_ref):
    del group_ref
    rows = x_ref.shape[0]
    per = LANES // order
    chunks = order // per
    output, inputs = output_ref[0], input_ref[0]
    bases = jnp.concatenate([output, output.T, inputs, inputs.T], axis=0)
    lane = lax.broadcasted_iota(jnp.int32, (order, order * order), 1)
    line = lax.broadcasted_iota(jnp.int32, (order, order * order), 0)
    spread = jnp.where(lane // order == line, 1.0, 0.0).astype(jnp.bfloat16)
    lane = lax.broadcasted_iota(jnp.int32, (order, LANES), 1)
    line = lax.broadcasted_iota(jnp.int32, (order, LANES), 0)
    repeat = jnp.where(lane % order == line, 1.0, 0.0).astype(jnp.bfloat16)

    first = 2 * order
    wide = mxu(jnp.concatenate(pieces(bases[:first], 3), axis=0), spread)
    wide = wide[:first] + wide[first : 2 * first] + wide[2 * first :]
    wide_out, wide_back = wide[:order], wide[order:]
    tall = mxu(jnp.concatenate(pieces(bases[first:], 2), axis=0), repeat)
    forward_high, back_high = tall[:order], tall[order : 2 * order]
    forward_low, back_low = tall[2 * order : 3 * order], tall[3 * order :]

    def placed(tile):
        blank = jnp.zeros_like(tile)
        return jnp.concatenate(
            [
                jnp.concatenate([tile if k == p else blank for k in range(per)], axis=0)
                for p in range(per)
            ],
            axis=1,
        ).astype(jnp.bfloat16)

    def mix(spread_rows, coefficients):
        totals = [jnp.zeros((rows, LANES), jnp.float32) for _ in range(chunks)]
        for c in range(chunks):
            for p in range(per):
                s = c * per + p
                value = spread_rows[c * rows : (c + 1) * rows, p * LANES : (p + 1) * LANES]
                for k in range(chunks):
                    weight = coefficients[s : s + 1, k * LANES : (k + 1) * LANES]
                    totals[k] = totals[k] + weight * value
        return totals

    x = x_ref[...].astype(jnp.float32)
    x = jnp.concatenate(
        [x[:, c * LANES : (c + 1) * LANES] for c in range(chunks)], axis=0
    ).astype(jnp.bfloat16)
    right = jnp.concatenate([placed(forward_high), placed(forward_low)], axis=0)
    rotated = mix(mxu(jnp.concatenate([x, x], axis=1), right), wide_out)

    eigen = eigen_ref[0]
    total = jnp.sum(jnp.sum(eigen, axis=1, keepdims=True), axis=0, keepdims=True)
    spectrum = eigen + damping_share * (total * (1.0 / (order * order)))
    scaled = jnp.concatenate(
        [rotated[k] / spectrum[k : k + 1] for k in range(chunks)], axis=0
    )
    high, low = pieces(scaled, 2)
    back = placed(back_high)
    restored = mxu(
        jnp.concatenate([high, low], axis=1), jnp.concatenate([back, back], axis=0)
    ) + mxu(high, placed(back_low))
    for k, total in enumerate(mix(restored, wide_back)):
        out_ref[:, k * LANES : (k + 1) * LANES] = total.astype(jnp.bfloat16)


def condition(queries, group_of, basis_out, basis_in, eigen):
    groups, order, _ = eigen.shape
    rows = queries.shape[0]
    size = order * order
    return pl.pallas_call(
        functools.partial(condition_kernel, order),
        grid_spec=pltpu.PrefetchScalarGridSpec(
            num_scalar_prefetch=1,
            grid=(groups,),
            in_specs=[
                pl.BlockSpec((rows, size), lambda b, g: (0, b)),
                pl.BlockSpec((1, order, order), lambda b, g: (g[b], 0, 0)),
                pl.BlockSpec((1, order, order), lambda b, g: (g[b], 0, 0)),
                pl.BlockSpec((1, size // LANES, LANES), lambda b, g: (g[b], 0, 0)),
            ],
            out_specs=pl.BlockSpec((rows, size), lambda b, g: (0, b)),
        ),
        out_shape=jax.ShapeDtypeStruct(queries.shape, jnp.bfloat16),
        compiler_params=pltpu.CompilerParams(vmem_limit_bytes=32 * 1024 * 1024),
        name="condition",
    )(group_of, queries, basis_out, basis_in, eigen.reshape(groups, size // LANES, LANES))


def arrange_kernel(scores_ref, ids_ref, out_ref, total):
    step = pl.program_id(0)
    taken, rows, count = scores_ref.shape
    groups = out_ref.shape[1] // WIDE
    ids = jnp.concatenate([ids_ref[k] for k in range(taken)], axis=1)
    coarse = ids // WIDE
    fine = ids % WIDE
    scores = jnp.concatenate([scores_ref[k] for k in range(taken)], axis=1).astype(
        jnp.float32
    )
    left = jnp.concatenate(
        [jnp.where(coarse == h, scores, 0.0) for h in range(groups)], axis=0
    ).astype(jnp.bfloat16)
    line = lax.broadcasted_iota(jnp.int32, (WIDE, taken * count), 0)
    chosen = jnp.where(line == fine, 1.0, 0.0).astype(jnp.bfloat16)
    term = lax.dot_general(
        left, chosen, (((1,), (1,)), ((), ())), preferred_element_type=jnp.float32
    )

    @pl.when(step == 0)
    def _():
        total[...] = term

    @pl.when(step > 0)
    def _():
        total[...] += term

    @pl.when(step == pl.num_programs(0) - 1)
    def _():
        for h in range(groups):
            out_ref[:, h * WIDE : (h + 1) * WIDE] = total[
                h * rows : (h + 1) * rows, :
            ].astype(jnp.bfloat16)


def arrange(parted, ids):
    blocks, rows, count = parted.shape
    width = blocks * count
    taken = 4 if blocks % 4 == 0 else 1
    return pl.pallas_call(
        arrange_kernel,
        grid=(blocks // taken,),
        in_specs=[
            pl.BlockSpec((taken, rows, count), lambda k: (k, 0, 0)),
            pl.BlockSpec((taken, 1, count), lambda k: (k, 0, 0)),
        ],
        out_specs=pl.BlockSpec((rows, width), lambda k: (0, 0)),
        out_shape=jax.ShapeDtypeStruct((rows, width), jnp.bfloat16),
        scratch_shapes=[pltpu.VMEM((rows * (width // WIDE), WIDE), jnp.float32)],
        compiler_params=pltpu.CompilerParams(vmem_limit_bytes=32 * 1024 * 1024),
        name="arrange",
    )(parted, ids.reshape(blocks, 1, count))


def ring_kernel(cores, x_ref, train_hbm, out_ref, held, train, total, stage, train_sem,
                ring_send, ring_recv, twin_send, twin_recv, back_send, back_recv,
                side_send, side_recv):
    blocks, rows, count = out_ref.shape
    half = rows // 2
    depth = x_ref.shape[1]
    chips = blocks // cores
    long = chips // 2
    third = (depth // 3 + WIDE // 2) // WIDE * WIDE
    slab = lax.axis_index("parts")
    step_rows = 4 * half
    pair = 2 * step_rows
    me = lax.axis_index("blk")
    core = me % cores
    chip = me // cores
    deep, side = chip // 2, chip % 2
    place = deep + side * (2 * long - 1 - 2 * deep)

    def device(position, its_core):
        at_side = position // long
        at_deep = position + at_side * (2 * long - 1 - 2 * position)
        return (at_deep * 2 + at_side) * cores + its_core

    onward = [device((place + 1) % chips, core), device((place + chips - 1) % chips, core)]
    twin = device(place, 1 - core)

    def columns_of(q):
        if q == 1:
            return pl.ds(2 * third, depth - 2 * third)
        start = slab if q == 0 else 1 - slab
        return pl.ds(pl.multiple_of(start * third, WIDE), third)

    def piece_of(u):
        if u == 4:
            return columns_of(2)
        if u < 2:
            size = third // 2
            return pl.ds(pl.multiple_of(slab * third + u * size, LANES), size)
        size = (depth - 2 * third) // 2
        return pl.ds(2 * third + (u - 2) * size, size)

    def rows_of(t, d, k):
        return pl.ds(pl.multiple_of((t * 4 + d * 2 + k) * half, half), half)

    def ring_copy(t, d, u):
        columns = piece_of(u)
        return pltpu.make_async_remote_copy(
            src_ref=held.at[rows_of(t, d, 0), columns],
            dst_ref=held.at[rows_of(t + 1, d, 0), columns],
            send_sem=ring_send.at[t, d, u],
            recv_sem=ring_recv.at[t, d, u],
            device_id={"blk": onward[d]},
            device_id_type=pl.DeviceIdType.MESH,
        )

    def twin_copy(t, d, u):
        columns = piece_of(u)
        return pltpu.make_async_remote_copy(
            src_ref=held.at[rows_of(t, d, 0), columns],
            dst_ref=held.at[rows_of(t, d, 1), columns],
            send_sem=twin_send.at[t, d, u],
            recv_sem=twin_recv.at[t, d, u],
            device_id={"blk": twin},
            device_id_type=pl.DeviceIdType.MESH,
        )

    def side_copy(t, d):
        columns = columns_of(0)
        return pltpu.make_async_remote_copy(
            src_ref=held.at[rows_of(t, d, 0), columns],
            dst_ref=held.at[rows_of(t, d, 0), columns],
            send_sem=side_send.at[t, d],
            recv_sem=side_recv.at[t, d],
            device_id={"parts": 1 - slab},
            device_id_type=pl.DeviceIdType.MESH,
        )

    def back_copy(t, d, k):
        shift = t if d == 1 else chips - t
        owner = device((place + shift) % chips, core if k == 0 else 1 - core)
        return pltpu.make_async_remote_copy(
            src_ref=stage.at[rows_of(t, d, k)],
            dst_ref=out_ref.at[me, pl.ds(d * half, half)],
            send_sem=back_send.at[t, d, k],
            recv_sem=back_recv.at[t, d, k],
            device_id={"blk": owner},
            device_id_type=pl.DeviceIdType.MESH,
        )

    load = pltpu.make_async_copy(train_hbm, train, train_sem)
    load.start()
    barrier = pltpu.get_barrier_semaphore()

    @pl.loop(1, blocks)
    def _(k):
        pl.semaphore_signal(
            barrier, inc=1, device_id={"blk": (me + k) % blocks},
            device_id_type=pl.DeviceIdType.MESH,
        )

    pl.semaphore_signal(
        barrier, inc=1, device_id={"parts": 1 - slab},
        device_id_type=pl.DeviceIdType.MESH,
    )
    for d in range(2):
        held[pl.ds(d * 2 * half, half), :] = x_ref[pl.ds(d * half, half), :]
    pl.semaphore_wait(barrier, blocks)

    def multiply(g, q, n):
        if n == 0:
            for step in range(2):
                for d in range(2):
                    for u in ((0, 1), (2, 3), (4,))[q]:
                        twin_copy(g * 2 + step, d, u).wait_recv()
        columns = columns_of(q)
        base = pl.ds(pl.multiple_of(g * pair, pair), pair)
        width = count // 2
        term = lax.dot_general(
            held[base, columns], train[n * width : (n + 1) * width, columns],
            (((1,), (1,)), ((), ())), preferred_element_type=jnp.float32,
        )
        sums = pl.ds(n * width, width)
        if q == 0:
            total[:, sums] = term
        elif q == 1:
            total[:, sums] += term
        else:
            stage[base, sums] = (total[:, sums] + term).astype(jnp.bfloat16)
        if q == 2 and n == 1:
            for step in range(2):
                for d in range(2):
                    for k in range(2):
                        if step == 0 and k == 0:

                            @pl.when(g > 0)
                            def _():
                                back_copy(g * 2 + step, d, k).start()

                        else:
                            back_copy(g * 2 + step, d, k).start()

    def from_side(t):
        for d in range(2):
            side_copy(t, d).wait_recv()
            twin_copy(t, d, 4).start()

    def forward(t, d, u):
        ring_copy(t, d, u).start()

    last = chips // 2 - 1

    @pl.loop(0, chips // 2)
    def _(g):
        for step in range(2):
            t = g * 2 + step
            for u in range(4):
                for d in range(2):
                    if step == 0:

                        @pl.when(g > 0)
                        def _():
                            ring_copy(t - 1, d, u).wait_recv()

                        forward(t, d, u)
                    else:
                        ring_copy(t - 1, d, u).wait_recv()

                        @pl.when(g < last)
                        def _():
                            forward(t, d, u)

                    if u == 1:
                        if step == 0:

                            @pl.when(g > 0)
                            def _():
                                side_copy(t, d).start()

                        else:
                            side_copy(t, d).start()
                    twin_copy(t, d, u).start()
                if step == 0:

                    @pl.when(g > 0)
                    def _():
                        if u == 0:

                            @pl.when(g == 1)
                            def _():
                                load.wait()

                        multiply(g - 1, u // 2, u % 2)

                elif u < 2:

                    @pl.when(g > 0)
                    def _():
                        multiply(g - 1, 2, u)

            if step == 0:

                @pl.when(g == 0)
                def _():
                    for d in range(2):
                        twin_copy(t, d, 4).start()

                @pl.when(g > 0)
                def _():
                    from_side(t - 1)

            else:

                @pl.when(g > 0)
                def _():
                    from_side(t - 1)

    for u in range(4):
        multiply(last, u // 2, u % 2)
    from_side(chips - 1)
    for n in range(2):
        multiply(last, 2, n)
    for d in range(2):
        out_ref[me, pl.ds(d * half, half), :] = stage[pl.ds(d * 2 * half, half), :]

    @pl.loop(0, chips)
    def _(t):
        for d in range(2):
            for u in range(5):
                twin_copy(t, d, u).wait_send()
            for u in range(4):

                @pl.when(t < chips - 1)
                def _():
                    ring_copy(t, d, u).wait_send()

            back_copy(t, d, 1).wait()

            @pl.when(t > 0)
            def _():
                side_copy(t, d).wait_send()
                back_copy(t, d, 0).wait()


def ring_scores(conditioned, train_grads, blocks, cores):
    rows, depth = conditioned.shape
    count = train_grads.shape[0]
    steps = blocks // cores
    return pl.pallas_call(
        functools.partial(ring_kernel, cores),
        out_shape=jax.ShapeDtypeStruct((blocks, rows, count), jnp.bfloat16),
        in_specs=[
            pl.BlockSpec(memory_space=pltpu.VMEM),
            pl.BlockSpec(memory_space=pl.ANY),
        ],
        out_specs=pl.BlockSpec(memory_space=pltpu.VMEM),
        scratch_shapes=[
            pltpu.VMEM((blocks * rows, depth), jnp.bfloat16),
            pltpu.VMEM((count, depth), jnp.bfloat16),
            pltpu.VMEM((4 * rows, count), jnp.float32),
            pltpu.VMEM((blocks * rows, count), jnp.bfloat16),
            pltpu.SemaphoreType.DMA,
            pltpu.SemaphoreType.DMA((steps, 2, 4)),
            pltpu.SemaphoreType.DMA((steps, 2, 4)),
            pltpu.SemaphoreType.DMA((steps, 2, 5)),
            pltpu.SemaphoreType.DMA((steps, 2, 5)),
            pltpu.SemaphoreType.DMA((steps, 2, 2)),
            pltpu.SemaphoreType.DMA((steps, 2, 2)),
            pltpu.SemaphoreType.DMA((steps, 2)),
            pltpu.SemaphoreType.DMA((steps, 2)),
        ],
        compiler_params=pltpu.CompilerParams(
            collective_id=0, has_side_effects=True, vmem_limit_bytes=56 * 1024 * 1024
        ),
        name="ring_scores",
    )(conditioned, train_grads)


def plain_scores(conditioned, train_grads):
    scores = lax.dot_general(
        lax.all_gather(conditioned, "blk", axis=0, tiled=True),
        train_grads,
        (((1,), (1,)), ((), ())),
        preferred_element_type=jnp.float32,
    ).astype(jnp.bfloat16)
    rows = conditioned.shape[0]
    return lax.all_to_all(
        scores.reshape(scores.shape[0] // rows, rows, scores.shape[1]),
        "blk",
        split_axis=0,
        concat_axis=0,
    )


def local(parts, blocks, queries, train_grads, group_of, basis_out, basis_in, eigen, store_ids):
    conditioned = condition(queries, group_of, basis_out, basis_in, eigen)
    if parts == 2 and blocks == 16 and queries.shape[0] % 32 == 0:
        parted = ring_scores(conditioned, train_grads, blocks, 2)
    else:
        parted = plain_scores(conditioned, train_grads)
    return arrange(parted, store_ids)


def solution(mesh):
    return jax.shard_map(
        functools.partial(local, mesh.shape["parts"], mesh.shape["blk"]),
        mesh=mesh,
        in_specs=(P("blk", None), P(("parts", "blk"), None), P(), P(), P(), P(), P("parts")),
        out_specs=P("blk", "parts"),
        check_vma=False,
    )
```

```python
import functools

import jax
import jax.numpy as jnp
from jax import lax
from jax.experimental import pallas as pl
from jax.experimental.pallas import tpu as pltpu
from jax.sharding import PartitionSpec as P

damping_share = 0.1
LANES = 128
WIDE = 256


def pieces(values, count):
    parts = []
    for _ in range(count):
        part = values.astype(jnp.bfloat16)
        parts.append(part)
        values = values - part.astype(jnp.float32)
    return parts


def mxu(left, right):
    return lax.dot_general(
        left, right, (((1,), (0,)), ((), ())), preferred_element_type=jnp.float32
    )


def condition_kernel(order, group_ref, x_ref, output_ref, input_ref, eigen_ref, out_ref):
    del group_ref
    rows = x_ref.shape[0]
    per = LANES // order
    chunks = order // per
    output, inputs = output_ref[0], input_ref[0]
    bases = jnp.concatenate([output, output.T, inputs, inputs.T], axis=0)
    lane = lax.broadcasted_iota(jnp.int32, (order, order * order), 1)
    line = lax.broadcasted_iota(jnp.int32, (order, order * order), 0)
    spread = jnp.where(lane // order == line, 1.0, 0.0).astype(jnp.bfloat16)
    lane = lax.broadcasted_iota(jnp.int32, (order, LANES), 1)
    line = lax.broadcasted_iota(jnp.int32, (order, LANES), 0)
    repeat = jnp.where(lane % order == line, 1.0, 0.0).astype(jnp.bfloat16)

    first = 2 * order
    wide = mxu(jnp.concatenate(pieces(bases[:first], 3), axis=0), spread)
    wide = wide[:first] + wide[first : 2 * first] + wide[2 * first :]
    wide_out, wide_back = wide[:order], wide[order:]
    tall = mxu(jnp.concatenate(pieces(bases[first:], 2), axis=0), repeat)
    forward_high, back_high = tall[:order], tall[order : 2 * order]
    forward_low, back_low = tall[2 * order : 3 * order], tall[3 * order :]

    def placed(tile):
        blank = jnp.zeros_like(tile)
        return jnp.concatenate(
            [
                jnp.concatenate([tile if k == p else blank for k in range(per)], axis=0)
                for p in range(per)
            ],
            axis=1,
        ).astype(jnp.bfloat16)

    def mix(spread_rows, coefficients):
        totals = [jnp.zeros((rows, LANES), jnp.float32) for _ in range(chunks)]
        for c in range(chunks):
            for p in range(per):
                s = c * per + p
                value = spread_rows[c * rows : (c + 1) * rows, p * LANES : (p + 1) * LANES]
                for k in range(chunks):
                    weight = coefficients[s : s + 1, k * LANES : (k + 1) * LANES]
                    totals[k] = totals[k] + weight * value
        return totals

    x = x_ref[...].astype(jnp.float32)
    x = jnp.concatenate(
        [x[:, c * LANES : (c + 1) * LANES] for c in range(chunks)], axis=0
    ).astype(jnp.bfloat16)
    right = jnp.concatenate([placed(forward_high), placed(forward_low)], axis=0)
    rotated = mix(mxu(jnp.concatenate([x, x], axis=1), right), wide_out)

    eigen = eigen_ref[0]
    total = jnp.sum(jnp.sum(eigen, axis=1, keepdims=True), axis=0, keepdims=True)
    spectrum = eigen + damping_share * (total * (1.0 / (order * order)))
    scaled = jnp.concatenate(
        [rotated[k] / spectrum[k : k + 1] for k in range(chunks)], axis=0
    )
    high, low = pieces(scaled, 2)
    back = placed(back_high)
    restored = mxu(
        jnp.concatenate([high, low], axis=1), jnp.concatenate([back, back], axis=0)
    ) + mxu(high, placed(back_low))
    for k, total in enumerate(mix(restored, wide_back)):
        out_ref[:, k * LANES : (k + 1) * LANES] = total.astype(jnp.bfloat16)


def condition(queries, group_of, basis_out, basis_in, eigen):
    groups, order, _ = eigen.shape
    rows = queries.shape[0]
    size = order * order
    return pl.pallas_call(
        functools.partial(condition_kernel, order),
        grid_spec=pltpu.PrefetchScalarGridSpec(
            num_scalar_prefetch=1,
            grid=(groups,),
            in_specs=[
                pl.BlockSpec((rows, size), lambda b, g: (0, b)),
                pl.BlockSpec((1, order, order), lambda b, g: (g[b], 0, 0)),
                pl.BlockSpec((1, order, order), lambda b, g: (g[b], 0, 0)),
                pl.BlockSpec((1, size // LANES, LANES), lambda b, g: (g[b], 0, 0)),
            ],
            out_specs=pl.BlockSpec((rows, size), lambda b, g: (0, b)),
        ),
        out_shape=jax.ShapeDtypeStruct(queries.shape, jnp.bfloat16),
        compiler_params=pltpu.CompilerParams(vmem_limit_bytes=32 * 1024 * 1024),
        name="condition",
    )(group_of, queries, basis_out, basis_in, eigen.reshape(groups, size // LANES, LANES))


def arrange_kernel(scores_ref, ids_ref, out_ref, total):
    step = pl.program_id(0)
    taken, rows, count = scores_ref.shape
    groups = out_ref.shape[1] // WIDE
    ids = jnp.concatenate([ids_ref[k] for k in range(taken)], axis=1)
    coarse = ids // WIDE
    fine = ids % WIDE
    scores = jnp.concatenate([scores_ref[k] for k in range(taken)], axis=1).astype(
        jnp.float32
    )
    left = jnp.concatenate(
        [jnp.where(coarse == h, scores, 0.0) for h in range(groups)], axis=0
    ).astype(jnp.bfloat16)
    line = lax.broadcasted_iota(jnp.int32, (WIDE, taken * count), 0)
    chosen = jnp.where(line == fine, 1.0, 0.0).astype(jnp.bfloat16)
    term = lax.dot_general(
        left, chosen, (((1,), (1,)), ((), ())), preferred_element_type=jnp.float32
    )

    @pl.when(step == 0)
    def _():
        total[...] = term

    @pl.when(step > 0)
    def _():
        total[...] += term

    @pl.when(step == pl.num_programs(0) - 1)
    def _():
        for h in range(groups):
            out_ref[:, h * WIDE : (h + 1) * WIDE] = total[
                h * rows : (h + 1) * rows, :
            ].astype(jnp.bfloat16)


def arrange(parted, ids):
    blocks, rows, count = parted.shape
    width = blocks * count
    taken = 4 if blocks % 4 == 0 else 1
    return pl.pallas_call(
        arrange_kernel,
        grid=(blocks // taken,),
        in_specs=[
            pl.BlockSpec((taken, rows, count), lambda k: (k, 0, 0)),
            pl.BlockSpec((taken, 1, count), lambda k: (k, 0, 0)),
        ],
        out_specs=pl.BlockSpec((rows, width), lambda k: (0, 0)),
        out_shape=jax.ShapeDtypeStruct((rows, width), jnp.bfloat16),
        scratch_shapes=[pltpu.VMEM((rows * (width // WIDE), WIDE), jnp.float32)],
        compiler_params=pltpu.CompilerParams(vmem_limit_bytes=32 * 1024 * 1024),
        name="arrange",
    )(parted, ids.reshape(blocks, 1, count))


def ring_kernel(cores, x_ref, train_hbm, out_ref, held, train, total, stage, train_sem,
                ring_send, ring_recv, twin_send, twin_recv, back_send, back_recv,
                side_send, side_recv):
    blocks, rows, count = out_ref.shape
    half = rows // 2
    depth = x_ref.shape[1]
    chips = blocks // cores
    long = chips // 2
    third = (depth // 3 + WIDE // 2) // WIDE * WIDE
    slab = lax.axis_index("parts")
    step_rows = 4 * half
    pair = 2 * step_rows
    me = lax.axis_index("blk")
    core = me % cores
    chip = me // cores
    deep, side = chip // 2, chip % 2
    place = deep + side * (2 * long - 1 - 2 * deep)

    def device(position, its_core):
        at_side = position // long
        at_deep = position + at_side * (2 * long - 1 - 2 * position)
        return (at_deep * 2 + at_side) * cores + its_core

    onward = [device((place + 1) % chips, core), device((place + chips - 1) % chips, core)]
    twin = device(place, 1 - core)

    def columns_of(q):
        if q == 1:
            return pl.ds(2 * third, depth - 2 * third)
        start = slab if q == 0 else 1 - slab
        return pl.ds(pl.multiple_of(start * third, WIDE), third)

    def piece_of(u):
        if u == 4:
            return columns_of(2)
        if u < 2:
            size = third // 2
            return pl.ds(pl.multiple_of(slab * third + u * size, LANES), size)
        size = (depth - 2 * third) // 2
        return pl.ds(2 * third + (u - 2) * size, size)

    def rows_of(t, d, k):
        return pl.ds(pl.multiple_of((t * 4 + d * 2 + k) * half, half), half)

    def ring_copy(t, d, u):
        columns = piece_of(u)
        return pltpu.make_async_remote_copy(
            src_ref=held.at[rows_of(t, d, 0), columns],
            dst_ref=held.at[rows_of(t + 1, d, 0), columns],
            send_sem=ring_send.at[t, d, u],
            recv_sem=ring_recv.at[t, d, u],
            device_id={"blk": onward[d]},
            device_id_type=pl.DeviceIdType.MESH,
        )

    def twin_copy(t, d, u):
        columns = piece_of(u)
        return pltpu.make_async_remote_copy(
            src_ref=held.at[rows_of(t, d, 0), columns],
            dst_ref=held.at[rows_of(t, d, 1), columns],
            send_sem=twin_send.at[t, d, u],
            recv_sem=twin_recv.at[t, d, u],
            device_id={"blk": twin},
            device_id_type=pl.DeviceIdType.MESH,
        )

    def side_copy(t, d):
        columns = columns_of(0)
        return pltpu.make_async_remote_copy(
            src_ref=held.at[rows_of(t, d, 0), columns],
            dst_ref=held.at[rows_of(t, d, 0), columns],
            send_sem=side_send.at[t, d],
            recv_sem=side_recv.at[t, d],
            device_id={"parts": 1 - slab},
            device_id_type=pl.DeviceIdType.MESH,
        )

    def back_copy(t, d, k):
        shift = t if d == 1 else chips - t
        owner = device((place + shift) % chips, core if k == 0 else 1 - core)
        return pltpu.make_async_remote_copy(
            src_ref=stage.at[rows_of(t, d, k)],
            dst_ref=out_ref.at[me, pl.ds(d * half, half)],
            send_sem=back_send.at[t, d, k],
            recv_sem=back_recv.at[t, d, k],
            device_id={"blk": owner},
            device_id_type=pl.DeviceIdType.MESH,
        )

    load = pltpu.make_async_copy(train_hbm, train, train_sem)
    load.start()
    barrier = pltpu.get_barrier_semaphore()

    @pl.loop(1, blocks)
    def _(k):
        pl.semaphore_signal(
            barrier, inc=1, device_id={"blk": (me + k) % blocks},
            device_id_type=pl.DeviceIdType.MESH,
        )

    pl.semaphore_signal(
        barrier, inc=1, device_id={"parts": 1 - slab},
        device_id_type=pl.DeviceIdType.MESH,
    )
    for d in range(2):
        held[pl.ds(d * 2 * half, half), :] = x_ref[pl.ds(d * half, half), :]
    pl.semaphore_wait(barrier, blocks)

    def multiply(g, q, n):
        if n == 0:
            for step in range(2):
                for d in range(2):
                    for u in ((0, 1), (2, 3), (4,))[q]:
                        twin_copy(g * 2 + step, d, u).wait_recv()
        columns = columns_of(q)
        base = pl.ds(pl.multiple_of(g * pair, pair), pair)
        width = count // 2
        term = lax.dot_general(
            train[n * width : (n + 1) * width, columns], held[base, columns],
            (((1,), (1,)), ((), ())), preferred_element_type=jnp.float32,
        )
        sums = pl.ds(n * width, width)
        if q == 0:
            total[sums, :] = term
        elif q == 1:
            total[sums, :] += term
        else:
            stage[base, sums] = (total[sums, :] + term).T.astype(jnp.bfloat16)
        if q == 2 and n == 1:
            for step in range(2):
                for d in range(2):
                    for k in range(2):
                        if step == 0 and k == 0:

                            @pl.when(g > 0)
                            def _():
                                back_copy(g * 2 + step, d, k).start()

                        else:
                            back_copy(g * 2 + step, d, k).start()

    def from_side(t):
        for d in range(2):
            side_copy(t, d).wait_recv()
            twin_copy(t, d, 4).start()

    def forward(t, d, u):
        ring_copy(t, d, u).start()

    last = chips // 2 - 1

    @pl.loop(0, chips // 2)
    def _(g):
        for step in range(2):
            t = g * 2 + step
            for u in range(4):
                for d in range(2):
                    if step == 0:

                        @pl.when(g > 0)
                        def _():
                            ring_copy(t - 1, d, u).wait_recv()

                        forward(t, d, u)
                    else:
                        ring_copy(t - 1, d, u).wait_recv()

                        @pl.when(g < last)
                        def _():
                            forward(t, d, u)

                    if u == 1:
                        if step == 0:

                            @pl.when(g > 0)
                            def _():
                                side_copy(t, d).start()

                        else:
                            side_copy(t, d).start()
                    twin_copy(t, d, u).start()
                if step == 0:

                    @pl.when(g > 0)
                    def _():
                        if u == 0:

                            @pl.when(g == 1)
                            def _():
                                load.wait()

                        multiply(g - 1, u // 2, u % 2)

                elif u < 2:

                    @pl.when(g > 0)
                    def _():
                        multiply(g - 1, 2, u)

            if step == 0:

                @pl.when(g == 0)
                def _():
                    for d in range(2):
                        twin_copy(t, d, 4).start()

                @pl.when(g > 0)
                def _():
                    from_side(t - 1)

            else:

                @pl.when(g > 0)
                def _():
                    from_side(t - 1)

    for u in range(4):
        multiply(last, u // 2, u % 2)
    from_side(chips - 1)
    for n in range(2):
        multiply(last, 2, n)
    for d in range(2):
        out_ref[me, pl.ds(d * half, half), :] = stage[pl.ds(d * 2 * half, half), :]

    @pl.loop(0, chips)
    def _(t):
        for d in range(2):
            for u in range(5):
                twin_copy(t, d, u).wait_send()
            for u in range(4):

                @pl.when(t < chips - 1)
                def _():
                    ring_copy(t, d, u).wait_send()

            back_copy(t, d, 1).wait()

            @pl.when(t > 0)
            def _():
                side_copy(t, d).wait_send()
                back_copy(t, d, 0).wait()


def ring_scores(conditioned, train_grads, blocks, cores):
    rows, depth = conditioned.shape
    count = train_grads.shape[0]
    steps = blocks // cores
    return pl.pallas_call(
        functools.partial(ring_kernel, cores),
        out_shape=jax.ShapeDtypeStruct((blocks, rows, count), jnp.bfloat16),
        in_specs=[
            pl.BlockSpec(memory_space=pltpu.VMEM),
            pl.BlockSpec(memory_space=pl.ANY),
        ],
        out_specs=pl.BlockSpec(memory_space=pltpu.VMEM),
        scratch_shapes=[
            pltpu.VMEM((blocks * rows, depth), jnp.bfloat16),
            pltpu.VMEM((count, depth), jnp.bfloat16),
            pltpu.VMEM((count, 4 * rows), jnp.float32),
            pltpu.VMEM((blocks * rows, count), jnp.bfloat16),
            pltpu.SemaphoreType.DMA,
            pltpu.SemaphoreType.DMA((steps, 2, 4)),
            pltpu.SemaphoreType.DMA((steps, 2, 4)),
            pltpu.SemaphoreType.DMA((steps, 2, 5)),
            pltpu.SemaphoreType.DMA((steps, 2, 5)),
            pltpu.SemaphoreType.DMA((steps, 2, 2)),
            pltpu.SemaphoreType.DMA((steps, 2, 2)),
            pltpu.SemaphoreType.DMA((steps, 2)),
            pltpu.SemaphoreType.DMA((steps, 2)),
        ],
        compiler_params=pltpu.CompilerParams(
            collective_id=0, has_side_effects=True, vmem_limit_bytes=56 * 1024 * 1024
        ),
        name="ring_scores",
    )(conditioned, train_grads)


def plain_scores(conditioned, train_grads):
    scores = lax.dot_general(
        lax.all_gather(conditioned, "blk", axis=0, tiled=True),
        train_grads,
        (((1,), (1,)), ((), ())),
        preferred_element_type=jnp.float32,
    ).astype(jnp.bfloat16)
    rows = conditioned.shape[0]
    return lax.all_to_all(
        scores.reshape(scores.shape[0] // rows, rows, scores.shape[1]),
        "blk",
        split_axis=0,
        concat_axis=0,
    )


def local(parts, blocks, queries, train_grads, group_of, basis_out, basis_in, eigen, store_ids):
    conditioned = condition(queries, group_of, basis_out, basis_in, eigen)
    if parts == 2 and blocks == 16 and queries.shape[0] % 32 == 0:
        parted = ring_scores(conditioned, train_grads, blocks, 2)
    else:
        parted = plain_scores(conditioned, train_grads)
    return arrange(parted, store_ids)


def solution(mesh):
    return jax.shard_map(
        functools.partial(local, mesh.shape["parts"], mesh.shape["blk"]),
        mesh=mesh,
        in_specs=(P("blk", None), P(("parts", "blk"), None), P(), P(), P(), P(), P("parts")),
        out_specs=P("blk", "parts"),
        check_vma=False,
    )
```

```python
import functools

import jax
import jax.numpy as jnp
from jax import lax
from jax.experimental import pallas as pl
from jax.experimental.pallas import tpu as pltpu
from jax.sharding import PartitionSpec as P

damping_share = 0.1
LANES = 128
WIDE = 256


def pieces(values, count):
    parts = []
    for _ in range(count):
        part = values.astype(jnp.bfloat16)
        parts.append(part)
        values = values - part.astype(jnp.float32)
    return parts


def mxu(left, right):
    return lax.dot_general(
        left, right, (((1,), (0,)), ((), ())), preferred_element_type=jnp.float32
    )


def condition_kernel(order, group_ref, x_ref, output_ref, input_ref, eigen_ref, out_ref):
    del group_ref
    rows = x_ref.shape[0]
    per = LANES // order
    chunks = order // per
    output, inputs = output_ref[0], input_ref[0]
    bases = jnp.concatenate([output, output.T, inputs, inputs.T], axis=0)
    lane = lax.broadcasted_iota(jnp.int32, (order, order * order), 1)
    line = lax.broadcasted_iota(jnp.int32, (order, order * order), 0)
    spread = jnp.where(lane // order == line, 1.0, 0.0).astype(jnp.bfloat16)
    lane = lax.broadcasted_iota(jnp.int32, (order, LANES), 1)
    line = lax.broadcasted_iota(jnp.int32, (order, LANES), 0)
    repeat = jnp.where(lane % order == line, 1.0, 0.0).astype(jnp.bfloat16)

    first = 2 * order
    wide = mxu(jnp.concatenate(pieces(bases[:first], 3), axis=0), spread)
    wide = wide[:first] + wide[first : 2 * first] + wide[2 * first :]
    wide_out, wide_back = wide[:order], wide[order:]
    tall = mxu(jnp.concatenate(pieces(bases[first:], 2), axis=0), repeat)
    forward_high, back_high = tall[:order], tall[order : 2 * order]
    forward_low, back_low = tall[2 * order : 3 * order], tall[3 * order :]

    def placed(tile):
        blank = jnp.zeros_like(tile)
        return jnp.concatenate(
            [
                jnp.concatenate([tile if k == p else blank for k in range(per)], axis=0)
                for p in range(per)
            ],
            axis=1,
        ).astype(jnp.bfloat16)

    def mix(spread_rows, coefficients):
        totals = [jnp.zeros((rows, LANES), jnp.float32) for _ in range(chunks)]
        for c in range(chunks):
            for p in range(per):
                s = c * per + p
                value = spread_rows[c * rows : (c + 1) * rows, p * LANES : (p + 1) * LANES]
                for k in range(chunks):
                    weight = coefficients[s : s + 1, k * LANES : (k + 1) * LANES]
                    totals[k] = totals[k] + weight * value
        return totals

    x = x_ref[...].astype(jnp.float32)
    x = jnp.concatenate(
        [x[:, c * LANES : (c + 1) * LANES] for c in range(chunks)], axis=0
    ).astype(jnp.bfloat16)
    right = jnp.concatenate([placed(forward_high), placed(forward_low)], axis=0)
    rotated = mix(mxu(jnp.concatenate([x, x], axis=1), right), wide_out)

    eigen = eigen_ref[0]
    total = jnp.sum(jnp.sum(eigen, axis=1, keepdims=True), axis=0, keepdims=True)
    spectrum = eigen + damping_share * (total * (1.0 / (order * order)))
    scaled = jnp.concatenate(
        [rotated[k] / spectrum[k : k + 1] for k in range(chunks)], axis=0
    )
    high, low = pieces(scaled, 2)
    back = placed(back_high)
    restored = mxu(
        jnp.concatenate([high, low], axis=1), jnp.concatenate([back, back], axis=0)
    ) + mxu(high, placed(back_low))
    for k, total in enumerate(mix(restored, wide_back)):
        out_ref[:, k * LANES : (k + 1) * LANES] = total.astype(jnp.bfloat16)


def condition(queries, group_of, basis_out, basis_in, eigen):
    groups, order, _ = eigen.shape
    rows = queries.shape[0]
    size = order * order
    return pl.pallas_call(
        functools.partial(condition_kernel, order),
        grid_spec=pltpu.PrefetchScalarGridSpec(
            num_scalar_prefetch=1,
            grid=(groups,),
            in_specs=[
                pl.BlockSpec((rows, size), lambda b, g: (0, b)),
                pl.BlockSpec((1, order, order), lambda b, g: (g[b], 0, 0)),
                pl.BlockSpec((1, order, order), lambda b, g: (g[b], 0, 0)),
                pl.BlockSpec((1, size // LANES, LANES), lambda b, g: (g[b], 0, 0)),
            ],
            out_specs=pl.BlockSpec((rows, size), lambda b, g: (0, b)),
        ),
        out_shape=jax.ShapeDtypeStruct(queries.shape, jnp.bfloat16),
        compiler_params=pltpu.CompilerParams(vmem_limit_bytes=32 * 1024 * 1024),
        name="condition",
    )(group_of, queries, basis_out, basis_in, eigen.reshape(groups, size // LANES, LANES))


def arrange_kernel(scores_ref, ids_ref, out_ref, total):
    step = pl.program_id(0)
    taken, rows, count = scores_ref.shape
    groups = out_ref.shape[1] // WIDE
    ids = jnp.concatenate([ids_ref[k] for k in range(taken)], axis=1)
    coarse = ids // WIDE
    fine = ids % WIDE
    scores = jnp.concatenate([scores_ref[k] for k in range(taken)], axis=1).astype(
        jnp.float32
    )
    left = jnp.concatenate(
        [jnp.where(coarse == h, scores, 0.0) for h in range(groups)], axis=0
    ).astype(jnp.bfloat16)
    line = lax.broadcasted_iota(jnp.int32, (WIDE, taken * count), 0)
    chosen = jnp.where(line == fine, 1.0, 0.0).astype(jnp.bfloat16)
    term = lax.dot_general(
        left, chosen, (((1,), (1,)), ((), ())), preferred_element_type=jnp.float32
    )

    @pl.when(step == 0)
    def _():
        total[...] = term

    @pl.when(step > 0)
    def _():
        total[...] += term

    @pl.when(step == pl.num_programs(0) - 1)
    def _():
        for h in range(groups):
            out_ref[:, h * WIDE : (h + 1) * WIDE] = total[
                h * rows : (h + 1) * rows, :
            ].astype(jnp.bfloat16)


def arrange(parted, ids):
    blocks, rows, count = parted.shape
    width = blocks * count
    taken = 4 if blocks % 4 == 0 else 1
    return pl.pallas_call(
        arrange_kernel,
        grid=(blocks // taken,),
        in_specs=[
            pl.BlockSpec((taken, rows, count), lambda k: (k, 0, 0)),
            pl.BlockSpec((taken, 1, count), lambda k: (k, 0, 0)),
        ],
        out_specs=pl.BlockSpec((rows, width), lambda k: (0, 0)),
        out_shape=jax.ShapeDtypeStruct((rows, width), jnp.bfloat16),
        scratch_shapes=[pltpu.VMEM((rows * (width // WIDE), WIDE), jnp.float32)],
        compiler_params=pltpu.CompilerParams(vmem_limit_bytes=32 * 1024 * 1024),
        name="arrange",
    )(parted, ids.reshape(blocks, 1, count))


def ring_kernel(cores, x_ref, train_hbm, out_ref, held, train, total, stage, train_sem,
                ring_send, ring_recv, twin_send, twin_recv, back_send, back_recv,
                side_send, side_recv):
    blocks, rows, count = out_ref.shape
    half = rows // 2
    depth = x_ref.shape[1]
    chips = blocks // cores
    long = chips // 2
    third = depth * 3 // 8 // WIDE * WIDE
    slab = lax.axis_index("parts")
    step_rows = 4 * half
    pair = 2 * step_rows
    me = lax.axis_index("blk")
    core = me % cores
    chip = me // cores
    deep, side = chip // 2, chip % 2
    place = deep + side * (2 * long - 1 - 2 * deep)

    def device(position, its_core):
        at_side = position // long
        at_deep = position + at_side * (2 * long - 1 - 2 * position)
        return (at_deep * 2 + at_side) * cores + its_core

    onward = [device((place + 1) % chips, core), device((place + chips - 1) % chips, core)]
    twin = device(place, 1 - core)

    def columns_of(q):
        if q == 1:
            return pl.ds(2 * third, depth - 2 * third)
        start = slab if q == 0 else 1 - slab
        return pl.ds(pl.multiple_of(start * third, WIDE), third)

    def piece_of(u):
        if u == 4:
            return columns_of(2)
        if u < 2:
            size = third // 2
            return pl.ds(pl.multiple_of(slab * third + u * size, LANES), size)
        size = (depth - 2 * third) // 2
        return pl.ds(2 * third + (u - 2) * size, size)

    def rows_of(t, d, k):
        return pl.ds(pl.multiple_of((t * 4 + d * 2 + k) * half, half), half)

    def ring_copy(t, d, u):
        columns = piece_of(u)
        return pltpu.make_async_remote_copy(
            src_ref=held.at[rows_of(t, d, 0), columns],
            dst_ref=held.at[rows_of(t + 1, d, 0), columns],
            send_sem=ring_send.at[t, d, u],
            recv_sem=ring_recv.at[t, d, u],
            device_id={"blk": onward[d]},
            device_id_type=pl.DeviceIdType.MESH,
        )

    def twin_copy(t, d, u):
        columns = piece_of(u)
        return pltpu.make_async_remote_copy(
            src_ref=held.at[rows_of(t, d, 0), columns],
            dst_ref=held.at[rows_of(t, d, 1), columns],
            send_sem=twin_send.at[t, d, u],
            recv_sem=twin_recv.at[t, d, u],
            device_id={"blk": twin},
            device_id_type=pl.DeviceIdType.MESH,
        )

    def side_copy(t, d):
        columns = columns_of(0)
        return pltpu.make_async_remote_copy(
            src_ref=held.at[rows_of(t, d, 0), columns],
            dst_ref=held.at[rows_of(t, d, 0), columns],
            send_sem=side_send.at[t, d],
            recv_sem=side_recv.at[t, d],
            device_id={"parts": 1 - slab},
            device_id_type=pl.DeviceIdType.MESH,
        )

    def back_copy(t, d, k):
        shift = t if d == 1 else chips - t
        owner = device((place + shift) % chips, core if k == 0 else 1 - core)
        return pltpu.make_async_remote_copy(
            src_ref=stage.at[rows_of(t, d, k)],
            dst_ref=out_ref.at[me, pl.ds(d * half, half)],
            send_sem=back_send.at[t, d, k],
            recv_sem=back_recv.at[t, d, k],
            device_id={"blk": owner},
            device_id_type=pl.DeviceIdType.MESH,
        )

    load = pltpu.make_async_copy(train_hbm, train, train_sem)
    load.start()
    barrier = pltpu.get_barrier_semaphore()

    @pl.loop(1, blocks)
    def _(k):
        pl.semaphore_signal(
            barrier, inc=1, device_id={"blk": (me + k) % blocks},
            device_id_type=pl.DeviceIdType.MESH,
        )

    pl.semaphore_signal(
        barrier, inc=1, device_id={"parts": 1 - slab},
        device_id_type=pl.DeviceIdType.MESH,
    )
    for d in range(2):
        held[pl.ds(d * 2 * half, half), :] = x_ref[pl.ds(d * half, half), :]
    pl.semaphore_wait(barrier, blocks)

    def multiply(g, q, n):
        if n == 0:
            for step in range(2):
                for d in range(2):
                    for u in ((0, 1), (2, 3), (4,))[q]:
                        twin_copy(g * 2 + step, d, u).wait_recv()
        columns = columns_of(q)
        base = pl.ds(pl.multiple_of(g * pair, pair), pair)
        width = count // 2
        term = lax.dot_general(
            held[base, columns], train[n * width : (n + 1) * width, columns],
            (((1,), (1,)), ((), ())), preferred_element_type=jnp.float32,
        )
        sums = pl.ds(n * width, width)
        if q == 0:
            total[:, sums] = term
        elif q == 1:
            total[:, sums] += term
        else:
            stage[base, sums] = (total[:, sums] + term).astype(jnp.bfloat16)
        if q == 2 and n == 1:
            for step in range(2):
                for d in range(2):
                    for k in range(2):
                        if step == 0 and k == 0:

                            @pl.when(g > 0)
                            def _():
                                back_copy(g * 2 + step, d, k).start()

                        else:
                            back_copy(g * 2 + step, d, k).start()

    def from_side(t):
        for d in range(2):
            side_copy(t, d).wait_recv()
            twin_copy(t, d, 4).start()

    def forward(t, d, u):
        ring_copy(t, d, u).start()

    last = chips // 2 - 1

    @pl.loop(0, chips // 2)
    def _(g):
        for step in range(2):
            t = g * 2 + step
            for u in range(4):
                for d in range(2):
                    if step == 0:

                        @pl.when(g > 0)
                        def _():
                            ring_copy(t - 1, d, u).wait_recv()

                        forward(t, d, u)
                    else:
                        ring_copy(t - 1, d, u).wait_recv()

                        @pl.when(g < last)
                        def _():
                            forward(t, d, u)

                    if u == 1:
                        if step == 0:

                            @pl.when(g > 0)
                            def _():
                                side_copy(t, d).start()

                        else:
                            side_copy(t, d).start()
                    twin_copy(t, d, u).start()
                if step == 0:

                    @pl.when(g > 0)
                    def _():
                        if u == 0:

                            @pl.when(g == 1)
                            def _():
                                load.wait()

                        multiply(g - 1, u // 2, u % 2)

                elif u < 2:

                    @pl.when(g > 0)
                    def _():
                        multiply(g - 1, 2, u)

            if step == 0:

                @pl.when(g == 0)
                def _():
                    for d in range(2):
                        twin_copy(t, d, 4).start()

                @pl.when(g > 0)
                def _():
                    from_side(t - 1)

            else:

                @pl.when(g > 0)
                def _():
                    from_side(t - 1)

    for u in range(4):
        multiply(last, u // 2, u % 2)
    from_side(chips - 1)
    for n in range(2):
        multiply(last, 2, n)
    for d in range(2):
        out_ref[me, pl.ds(d * half, half), :] = stage[pl.ds(d * 2 * half, half), :]

    @pl.loop(0, chips)
    def _(t):
        for d in range(2):
            for u in range(5):
                twin_copy(t, d, u).wait_send()
            for u in range(4):

                @pl.when(t < chips - 1)
                def _():
                    ring_copy(t, d, u).wait_send()

            back_copy(t, d, 1).wait()

            @pl.when(t > 0)
            def _():
                side_copy(t, d).wait_send()
                back_copy(t, d, 0).wait()


def ring_scores(conditioned, train_grads, blocks, cores):
    rows, depth = conditioned.shape
    count = train_grads.shape[0]
    steps = blocks // cores
    return pl.pallas_call(
        functools.partial(ring_kernel, cores),
        out_shape=jax.ShapeDtypeStruct((blocks, rows, count), jnp.bfloat16),
        in_specs=[
            pl.BlockSpec(memory_space=pltpu.VMEM),
            pl.BlockSpec(memory_space=pl.ANY),
        ],
        out_specs=pl.BlockSpec(memory_space=pltpu.VMEM),
        scratch_shapes=[
            pltpu.VMEM((blocks * rows, depth), jnp.bfloat16),
            pltpu.VMEM((count, depth), jnp.bfloat16),
            pltpu.VMEM((4 * rows, count), jnp.float32),
            pltpu.VMEM((blocks * rows, count), jnp.bfloat16),
            pltpu.SemaphoreType.DMA,
            pltpu.SemaphoreType.DMA((steps, 2, 4)),
            pltpu.SemaphoreType.DMA((steps, 2, 4)),
            pltpu.SemaphoreType.DMA((steps, 2, 5)),
            pltpu.SemaphoreType.DMA((steps, 2, 5)),
            pltpu.SemaphoreType.DMA((steps, 2, 2)),
            pltpu.SemaphoreType.DMA((steps, 2, 2)),
            pltpu.SemaphoreType.DMA((steps, 2)),
            pltpu.SemaphoreType.DMA((steps, 2)),
        ],
        compiler_params=pltpu.CompilerParams(
            collective_id=0, has_side_effects=True, vmem_limit_bytes=56 * 1024 * 1024
        ),
        name="ring_scores",
    )(conditioned, train_grads)


def plain_scores(conditioned, train_grads):
    scores = lax.dot_general(
        lax.all_gather(conditioned, "blk", axis=0, tiled=True),
        train_grads,
        (((1,), (1,)), ((), ())),
        preferred_element_type=jnp.float32,
    ).astype(jnp.bfloat16)
    rows = conditioned.shape[0]
    return lax.all_to_all(
        scores.reshape(scores.shape[0] // rows, rows, scores.shape[1]),
        "blk",
        split_axis=0,
        concat_axis=0,
    )


def local(parts, blocks, queries, train_grads, group_of, basis_out, basis_in, eigen, store_ids):
    conditioned = condition(queries, group_of, basis_out, basis_in, eigen)
    if parts == 2 and blocks == 16 and queries.shape[0] % 32 == 0:
        parted = ring_scores(conditioned, train_grads, blocks, 2)
    else:
        parted = plain_scores(conditioned, train_grads)
    return arrange(parted, store_ids)


def solution(mesh):
    return jax.shard_map(
        functools.partial(local, mesh.shape["parts"], mesh.shape["blk"]),
        mesh=mesh,
        in_specs=(P("blk", None), P(("parts", "blk"), None), P(), P(), P(), P(), P("parts")),
        out_specs=P("blk", "parts"),
        check_vma=False,
    )
```
